256 devices in a mesh: island: 32 (over y, x, core), shard: 8 (over z).
Axes of the slice: x: 4, y: 4, z: 8, core: 2. Of those that a mesh axis runs over, the one named last changes fastest.
Arguments:
- pseudo_grad: bfloat16 [32, 2, 2048, 2048], P('island', None, None, 'shard'), may hold values from -4 to 4
- path_table: int32 [32, 2], replicated, may hold values from 0 to 15
- owner_place: int32 [32], replicated, may hold values from 0 to 31, each once
- outer_param: float32 [32, 2048, 2048], P('island', 'shard'), may hold values from -4 to 4
- outer_momentum: float32 [32, 2048, 2048], P('island', 'shard'), may hold values from -3 to 3
Outputs:
- new_param: float32 [32, 2048, 2048], P('island', 'shard')
- new_momentum: float32 [32, 2048, 2048], P('island', 'shard')
- returned: bfloat16 [32, 2, 2048, 2048], P('island', None, None, 'shard')
The draws below stay inside these ranges and needn't reach their ends.
Inputs may be any that keep to these rules, and one draw needn't show every extreme that they name: `path_table`: entry [i, l] picks module l * 16 + entry of level l for island i. Each value appears once; module m's outer state is row owner_place[m] of outer_param and outer_momentum.
All inputs are finite; a program needn't handle non-finite values.
Results may differ from the reference program's by a relative error of at most 0.001.
Values may be sent and summed in bfloat16 or wider, within the bound.
No kernel may reach another device: no remote copies, remote signals or barrier semaphores. Data moves between devices by JAX's collectives and lax.ppermute only.
A program may use at most 128 MiB of HBM per device.

```python
import math
import jax
import jax.numpy as jnp
import numpy as np
from jax import lax

D = 2048
LEVELS = 2
ROWS = 2048
ISLANDS = 32
MODULES = 32
MODS = 16


def set_ends(entries, rng, smallest, largest):
    longest = entries.shape.index(max(entries.shape))
    spots = []
    for shift in (0, 1):
        where = [jax.random.randint(jax.random.fold_in(rng, axis), (), 0, length) for axis, length in enumerate(entries.shape)]
        where[longest] = (where[longest] + shift) % entries.shape[longest]
        spots.append(tuple(where))
    return entries.at[spots[0]].set(smallest).at[spots[1]].set(largest)


def level_of(key, dims, shards, low, top_value):
    def one(dim, parts):
        draws = jax.random.uniform(jax.random.fold_in(jax.random.fold_in(key, 6), dim), (parts,), jnp.float32, low / len(shards), top_value / len(shards))
        return jnp.repeat(jnp.exp(draws), dims[dim] // parts).reshape((-1,) + (1,) * (len(dims) - dim - 1))

    gain = one(*shards[0])
    for cut in shards[1:]:
        gain = gain * one(*cut)
    return gain


def cumulative_ranks(count, skew):
    weights = [(1 << 20) // math.isqrt(rank ** skew) + 1 for rank in range(1, count + 1)]
    deviation = 1 + sum(weights) // (1 << 30)
    return np.cumsum(np.array([max(1, weight // deviation) for weight in weights]))


def ranked_ids(rng, extent, number_of, lean):
    grid = cumulative_ranks(number_of, lean)
    lot = jax.random.randint(jax.random.fold_in(rng, 1), extent, 0, int(grid[number_of - 1]))
    standing = jnp.searchsorted(jnp.asarray(grid, jnp.int32), lot, side="right")
    return jax.random.permutation(jax.random.fold_in(rng, 2), number_of)[standing].astype(jnp.int32)


def gaussian(key, shape, width, most, pieces=(), held_as=jnp.bfloat16):
    entries = jax.random.normal(key, shape, jnp.float32) * width
    if len(pieces) > 0:
        entries = level_of(key, shape, pieces, -0.22, 0.18) * entries
    return jnp.clip(entries, min=-most, max=most).astype(held_as)


def setup_inputs(seed: int = 0) -> dict:
    key_of = jax.random.split(jax.random.key(seed), 6)
    pseudo_grad = gaussian(key_of[0], (ISLANDS, LEVELS, ROWS, D), 0.5, 4.0, ((0, 32), (3, 8)))
    path_table = set_ends(ranked_ids(key_of[1], (ISLANDS, LEVELS), MODS, 2), jax.random.fold_in(key_of[1], 3), 0, MODS - 1).astype(jnp.int32)
    owner_place = jax.random.permutation(key_of[2], MODULES).astype(jnp.int32)
    outer_param = gaussian(key_of[3], (MODULES, ROWS, D), 0.5, 4.0, ((0, 32), (1, 8)), jnp.float32)
    outer_momentum = gaussian(key_of[4], (MODULES, ROWS, D), 0.3, 3.0, ((0, 32), (1, 8)), jnp.float32)
    return dict(pseudo_grad=pseudo_grad, path_table=path_table, owner_place=owner_place, outer_param=outer_param, outer_momentum=outer_momentum)


def reference(pseudo_grad, path_table, owner_place, outer_param, outer_momentum):
    module_ids = jnp.arange(LEVELS, dtype=jnp.int32)[None, :] * MODS + path_table
    target = jnp.take(owner_place, module_ids.reshape(-1), axis=0).astype(jnp.int32)
    flattened = pseudo_grad.reshape(ISLANDS * LEVELS, ROWS, D)

    def accumulate(running, pair):
        target_row, pseudo = pair
        return running.at[target_row].add(pseudo.astype(jnp.float32)), None

    totals, _ = lax.scan(accumulate, jnp.zeros((MODULES, ROWS, D), jnp.float32), (target, flattened))
    member = target[None, :] == jnp.arange(MODULES, dtype=jnp.int32)[:, None]
    counts = jnp.sum(member.astype(jnp.float32), axis=1)
    mean_grad = totals / jnp.maximum(counts, 1.0)[:, None, None]
    new_momentum = 0.9 * outer_momentum + mean_grad
    new_param = outer_param - 0.7 * (mean_grad + 0.9 * new_momentum)
    returned = jnp.take(new_param.astype(jnp.bfloat16), target, axis=0).reshape(ISLANDS, LEVELS, ROWS, D)
    return new_param, new_momentum, returned
```

```python
import functools

import jax
import jax.numpy as jnp
from jax import lax
from jax.experimental import pallas as pl
from jax.experimental.pallas import tpu as pltpu
from jax.sharding import PartitionSpec as P

LEARN_RATE = 0.7
MOMENTUM_COEF = 0.9
Q_COEF = LEARN_RATE * MOMENTUM_COEF * MOMENTUM_COEF
G_COEF = LEARN_RATE * (1.0 + MOMENTUM_COEF)
TR, TC = 16, 128
VMEM_LIMIT = 32 * 1024 * 1024

SMEM = pl.BlockSpec(memory_space=pltpu.SMEM)
VMEM = pl.BlockSpec(memory_space=pltpu.VMEM)


def call(kernel, out_shape, in_specs, out_specs, scratch=(), grid=None, moved=0):
    extra = {} if grid is None else {"grid": grid}
    return pl.pallas_call(
        kernel,
        out_shape=out_shape,
        in_specs=in_specs,
        out_specs=out_specs,
        scratch_shapes=scratch,
        compiler_params=pltpu.CompilerParams(vmem_limit_bytes=VMEM_LIMIT),
        cost_estimate=pl.CostEstimate(flops=moved, bytes_accessed=moved, transcendentals=0),
        **extra,
    )


def tiles(*lead, dtype=jnp.bfloat16):
    return jax.ShapeDtypeStruct((*lead, TR, TC), dtype)


def pack_by_shard(n, zr, jrs, jcs, me_ref, x_ref, *outs):
    me = me_ref[0]
    for k in range(n):
        z = lax.rem(me + k, n)
        for jr in range(jrs):
            rows = pl.ds(pl.multiple_of(z * zr + jr * TR, TR), TR)
            for jc in range(jcs):
                outs[k][jr * jcs + jc] = x_ref[0, 0, rows, jc * TC : (jc + 1) * TC]


def pack_by_island(n, zr, jrs, jcs, x_ref, out_ref):
    for z in range(n):
        for jr in range(jrs):
            r0 = z * zr + jr * TR
            for jc in range(jcs):
                out_ref[jr * jcs + jc, z] = x_ref[0, 0, r0 : r0 + TR, jc * TC : (jc + 1) * TC]


def split_by_shard(n, count, me_ref, y_ref, *outs):
    me = me_ref[0]
    for k in range(n):
        z = lax.rem(me + k, n)
        for i in range(count):
            outs[k][i] = y_ref[i, z]


def join_by_shard(n, count, me_ref, *refs):
    me = me_ref[0]
    out_ref = refs[n]
    for k in range(n):
        s = lax.rem(me + n - k, n)
        for i in range(count):
            out_ref[i, s] = refs[k][i]


def q_kernel(n, jrs, jcs, p_ref, m_ref, out_ref):
    for jr in range(jrs):
        for s in range(n):
            for jc in range(jcs):
                rows = slice(jr * TR, (jr + 1) * TR)
                c0 = s * jcs * TC + jc * TC
                cols = slice(c0, c0 + TC)
                out_ref[jr * jcs + jc, s] = p_ref[0, rows, cols] - Q_COEF * m_ref[0, rows, cols]


def update_kernel(n, jrs, jcs, g_ref, p_ref, m_ref, np_ref, nm_ref):
    for jr in range(jrs):
        for s in range(n):
            for jc in range(jcs):
                rows = slice(jr * TR, (jr + 1) * TR)
                c0 = s * jcs * TC + jc * TC
                cols = slice(c0, c0 + TC)
                g = g_ref[jr * jcs + jc, s]
                nm = MOMENTUM_COEF * m_ref[0, rows, cols] + g
                nm_ref[0, rows, cols] = nm
                np_ref[0, rows, cols] = p_ref[0, rows, cols] - LEARN_RATE * (g + MOMENTUM_COEF * nm)


def reduce_kernel(n, islands, per_level, level, split, me_ref, path_ref, owner_ref, q_ref, *refs):
    me = me_ref[0]
    if split:
        grads, refs = refs[:n], refs[n:]
    else:
        grads, refs = refs[0], refs[1:]
    other = None
    if level == 0:
        other, refs = refs[0], refs[1:]
    mean_ref, outs, acc, cnt = refs[0], refs[1 : n + 1], refs[n + 1], refs[n + 2]
    acc[...] = jnp.zeros_like(acc)
    for m in range(per_level):
        cnt[m] = 0

    def add(i, carry):
        m = path_ref[i, level]
        cnt[m] = cnt[m] + 1
        for k in range(n):
            if split:
                s = lax.rem(me + n - k, n)
                acc[m, s] += grads[k][i].astype(jnp.float32)
            else:
                acc[m, k] += grads[i, k].astype(jnp.float32)
        return carry

    lax.fori_loop(0, islands, add, 0)

    def finish(m, carry):
        t = owner_ref[level * per_level + m]
        share = jnp.full((TR, TC), 1.0, jnp.float32) / jnp.maximum(cnt[m], 1).astype(jnp.float32)
        row = m if level else t
        for k in range(n):
            s = lax.rem(me + k, n)
            g = acc[m, s] * share
            mean_ref[row, s] = g
            outs[k][m] = (q_ref[t, s] - G_COEF * g).astype(jnp.bfloat16)
        if other is not None:
            row = owner_ref[per_level + m]
            for s in range(n):
                mean_ref[row, s] = other[m, s]
        return carry

    lax.fori_loop(0, per_level, finish, 0)


def pick_kernel(n, islands, levels, me_ref, path_ref, *refs):
    me = me_ref[0]
    out_ref = refs[levels * n]

    def one(i, carry):
        for l in range(levels):
            m = path_ref[i, l]
            for k in range(n):
                out_ref[i, l, lax.rem(me + n - k, n)] = refs[l * n + k][m]
        return carry

    lax.fori_loop(0, islands, one, 0)


def unpack_kernel(n, zr, jrs, jcs, levels, y_ref, out_ref):
    for l in range(levels):
        for z in range(n):
            for jr in range(jrs):
                r0 = z * zr + jr * TR
                for jc in range(jcs):
                    out_ref[0, l, r0 : r0 + TR, jc * TC : (jc + 1) * TC] = y_ref[jr * jcs + jc, l, z]


def body(pseudo_grad, path_table, owner_place, outer_param, outer_momentum):
    islands = lax.axis_size("island")
    n = lax.axis_size("shard")
    levels, full_rows, narrow = pseudo_grad.shape[1:]
    modules = owner_place.shape[0]
    per_level = modules // levels
    zr, width = outer_param.shape[1:]
    jrs, jcs = zr // TR, narrow // TC
    me = lax.axis_index("shard").astype(jnp.int32).reshape(1)

    def swap(x):
        return lax.all_to_all(x, "island", 0, 0, tiled=True)

    def shift(arrays):
        return [arrays[0]] + [
            lax.ppermute(arrays[k], "shard", [(i, (i + k) % n) for i in range(n)]) for k in range(1, n)
        ]

    def level_spec(l):
        return pl.BlockSpec((1, 1, full_rows, narrow), lambda g: (0, l, 0, 0))

    def whole(shape):
        return pl.BlockSpec(shape, lambda g: (0,) * len(shape))

    part = (islands, TR, TC)
    packed1 = call(
        functools.partial(pack_by_island, n, zr, jrs, jcs),
        tiles(islands, n),
        [level_spec(1)],
        whole((islands, n, TR, TC)),
        grid=(1,),
        moved=1 << 21,
    )(pseudo_grad)
    there1 = swap(packed1)
    parts0 = call(
        functools.partial(pack_by_shard, n, zr, jrs, jcs),
        [tiles(islands)] * n,
        [SMEM, level_spec(0)],
        [whole(part)] * n,
        grid=(1,),
        moved=1 << 21,
    )(me, pseudo_grad)
    parts0 = shift(parts0)

    steps = 4
    band = pl.BlockSpec((1, zr // steps, width), lambda g: (0, g, 0))
    tile_band = pl.BlockSpec((islands // steps, n, TR, TC), lambda g: (g, 0, 0, 0))
    q = call(
        functools.partial(q_kernel, n, jrs // steps, jcs),
        tiles(islands, n, dtype=jnp.float32),
        [band, band],
        tile_band,
        grid=(steps,),
        moved=6 << 20,
    )(outer_param, outer_momentum)
    q = swap(q)

    parts1 = call(
        functools.partial(split_by_shard, n, islands),
        [tiles(islands)] * n,
        [SMEM, VMEM],
        [VMEM] * n,
        moved=1 << 21,
    )(me, there1)
    parts1 = shift(parts1)

    joined0 = call(
        functools.partial(join_by_shard, n, islands),
        tiles(islands, n),
        [SMEM] + [VMEM] * n,
        VMEM,
        moved=1 << 21,
    )(me, *parts0)
    grads0 = swap(joined0)

    scratch = (pltpu.VMEM((per_level, n, TR, TC), jnp.float32), pltpu.SMEM((per_level,), jnp.int32))
    mean1, *new1 = call(
        functools.partial(reduce_kernel, n, islands, per_level, 1, True),
        [tiles(per_level, n, dtype=jnp.float32)] + [tiles(per_level)] * n,
        [SMEM] * 3 + [VMEM] * (n + 1),
        [VMEM] * (n + 1),
        scratch,
        moved=1 << 22,
    )(me, path_table, owner_place, q, *parts1)
    new1 = shift(new1)
    mean, *new0 = call(
        functools.partial(reduce_kernel, n, islands, per_level, 0, False),
        [tiles(modules, n, dtype=jnp.float32)] + [tiles(per_level)] * n,
        [SMEM] * 3 + [VMEM] * 3,
        [VMEM] * (n + 1),
        scratch,
        moved=1 << 22,
    )(me, path_table, owner_place, q, grads0, mean1)
    mean = swap(mean)
    new0 = shift(new0)

    picked = call(
        functools.partial(pick_kernel, n, islands, levels),
        tiles(islands, levels, n),
        [SMEM] * 2 + [VMEM] * (levels * n),
        VMEM,
        moved=1 << 22,
    )(me, path_table, *new0, *new1)
    arrived = swap(picked)

    new_param, new_momentum = call(
        functools.partial(update_kernel, n, jrs // steps, jcs),
        [jax.ShapeDtypeStruct(outer_param.shape, jnp.float32)] * 2,
        [tile_band, band, band],
        [band, band],
        grid=(steps,),
        moved=10 << 20,
    )(mean, outer_param, outer_momentum)
    returned = call(
        functools.partial(unpack_kernel, n, zr, jrs, jcs, levels),
        jax.ShapeDtypeStruct(pseudo_grad.shape, jnp.bfloat16),
        [VMEM],
        VMEM,
        moved=1 << 22,
    )(arrived)
    return new_param, new_momentum, returned


def solution(mesh):
    placed = (
        P("island", None, None, "shard"),
        P(),
        P(),
        P("island", "shard", None),
        P("island", "shard", None),
    )
    return jax.shard_map(
        body,
        mesh=mesh,
        in_specs=placed,
        out_specs=(
            P("island", "shard", None),
            P("island", "shard", None),
            P("island", None, None, "shard"),
        ),
        check_vma=False,
    )
```

```python
import functools

import jax
import jax.numpy as jnp
from jax import lax
from jax.experimental import pallas as pl
from jax.experimental.pallas import tpu as pltpu
from jax.sharding import PartitionSpec as P

LEARN_RATE = 0.7
MOMENTUM_COEF = 0.9
Q_COEF = LEARN_RATE * MOMENTUM_COEF * MOMENTUM_COEF
G_COEF = LEARN_RATE * (1.0 + MOMENTUM_COEF)
LEAST = 1e-30
LIMIT = 32000.0
STEPS = 8.0
TR, TC = 16, 128
VMEM_LIMIT = 60 * 1024 * 1024

SMEM = pl.BlockSpec(memory_space=pltpu.SMEM)
VMEM = pl.BlockSpec(memory_space=pltpu.VMEM)
AFTER = pl.BlockSpec(memory_space=pl.ANY)


def call(kernel, out_shape, in_specs, out_specs, scratch=(), grid=None, moved=0):
    extra = {} if grid is None else {"grid": grid}
    return pl.pallas_call(
        kernel,
        out_shape=out_shape,
        in_specs=in_specs,
        out_specs=out_specs,
        scratch_shapes=scratch,
        compiler_params=pltpu.CompilerParams(vmem_limit_bytes=VMEM_LIMIT),
        cost_estimate=pl.CostEstimate(flops=moved, bytes_accessed=moved, transcendentals=0),
        **extra,
    )


def tiles(*lead, dtype=jnp.bfloat16):
    return jax.ShapeDtypeStruct((*lead, TR, TC), dtype)


def pack_kernel(jrs, jcs, levels, x_ref, out_ref):
    for l in range(levels):
        for jr in range(jrs):
            rows = slice(jr * TR, (jr + 1) * TR)
            for jc in range(jcs):
                out_ref[jr * jcs + jc, 0, l] = x_ref[0, l, rows, jc * TC : (jc + 1) * TC]


def unpack_kernel(jrs, jcs, levels, y_ref, out_ref):
    for l in range(levels):
        for jr in range(jrs):
            rows = slice(jr * TR, (jr + 1) * TR)
            for jc in range(jcs):
                out_ref[0, l, rows, jc * TC : (jc + 1) * TC] = y_ref[jr * jcs + jc, 0, l]


def store_coded(out, n, values):
    top = functools.reduce(jnp.maximum, [jnp.abs(v) for v in values])
    octave = jnp.ceil(jnp.log2(jnp.maximum(top, LEAST)) * STEPS)
    gain = LIMIT * jnp.exp2(octave * (-1.0 / STEPS))
    for s, v in enumerate(values):
        out[s] = jnp.round(v * gain).astype(jnp.int32).astype(jnp.int16)
    out[n] = octave.astype(jnp.int32).astype(jnp.int16)


def scale_of(code):
    return jnp.exp2(code.astype(jnp.int32).astype(jnp.float32) * (1.0 / STEPS)) * (1.0 / LIMIT)


def decoded(code, scale):
    return code.astype(jnp.int32).astype(jnp.float32) * scale


CORES, SIDE = 2, 4


def place(at_ref):
    at = at_ref[0]
    return at % CORES, at // CORES % SIDE, at // (CORES * SIDE)


def towards(at_ref, emit):
    core, x, _ = place(at_ref)
    for y in range(SIDE):
        for d in range(SIDE):
            emit(d, y, y, lax.rem(x + d, SIDE), core)
            emit(SIDE, y * SIDE + d, y, d, 1 - core)


def q_kernel(n, jcs, at_ref, p_ref, m_ref, *outs):
    def emit(d, slot, y, x, core):
        rows = pl.ds(pl.multiple_of((y * SIDE + x) * TR, TR), TR)
        cols = [pl.ds(pl.multiple_of((s * jcs + core) * TC, TC), TC) for s in range(n)]
        store_coded(outs[d].at[slot], n, [p_ref[0, rows, c] - Q_COEF * m_ref[0, rows, c] for c in cols])

    towards(at_ref, emit)


def update_kernel(n, jrs, jcs, g_ref, p_ref, m_ref, np_ref, nm_ref):
    for jr in range(jrs):
        rows = slice(jr * TR, (jr + 1) * TR)
        for jc in range(jcs):
            j = jr * jcs + jc
            scale = scale_of(g_ref[j, n])
            for s in range(n):
                cols = slice((s * jcs + jc) * TC, (s * jcs + jc + 1) * TC)
                g = decoded(g_ref[j, s], scale)
                nm = MOMENTUM_COEF * m_ref[0, rows, cols] + g
                nm_ref[0, rows, cols] = nm
                np_ref[0, rows, cols] = p_ref[0, rows, cols] - LEARN_RATE * (g + MOMENTUM_COEF * nm)


def reduce_kernel(n, islands, levels, per_level, path_ref, owner_ref, q_ref, x_ref, sum_ref, pick_ref, new, cnt):
    sum_ref[...] = jnp.zeros_like(sum_ref)
    for m in range(levels * per_level):
        cnt[m] = 0

    def add(i, carry):
        for l in range(levels):
            m = l * per_level + path_ref[i, l]
            cnt[m] = cnt[m] + 1
            for s in range(n):
                sum_ref[m, s] += x_ref[i, s, l].astype(jnp.float32)
        return carry

    lax.fori_loop(0, islands, add, 0)

    def finish(m, carry):
        t = owner_ref[m]
        share = jnp.full((TR, TC), 1.0, jnp.float32) / jnp.maximum(cnt[m], 1).astype(jnp.float32)
        scale = scale_of(q_ref[t, n])
        for s in range(n):
            g = sum_ref[m, s] * share
            sum_ref[m, s] = g
            new[m, s] = (decoded(q_ref[t, s], scale) - G_COEF * g).astype(jnp.bfloat16)
        return carry

    lax.fori_loop(0, levels * per_level, finish, 0)

    def pick(i, carry):
        for l in range(levels):
            m = l * per_level + path_ref[i, l]
            for s in range(n):
                pick_ref[i, s, l] = new[m, s]
        return carry

    lax.fori_loop(0, islands, pick, 0)


def mean_kernel(n, modules, at_ref, owner_ref, sum_ref, *refs):
    outs, module = refs[: SIDE + 1], refs[SIDE + 1]
    for m in range(modules):
        module[owner_ref[m]] = m

    def emit(d, slot, y, x, core):
        m = module[(y * SIDE + x) * CORES + core]
        store_coded(outs[d].at[slot], n, [sum_ref[m, s] for s in range(n)])

    towards(at_ref, emit)


def split_other(at_ref, other_ref, *outs):
    _, _, y = place(at_ref)
    for d in range(SIDE):
        for x in range(SIDE):
            outs[d][x] = other_ref[lax.rem(y + d, SIDE) * SIDE + x]


def turn(across, at_ref, *refs):
    ins, outs = refs[:SIDE], refs[SIDE:]
    mine = place(at_ref)[across]
    for d in range(SIDE):
        for e in range(SIDE):
            outs[d][e] = ins[e][lax.rem(mine + d, SIDE)]


def join_all(at_ref, *refs):
    same, other, out_ref = refs[:SIDE], refs[SIDE : 2 * SIDE], refs[2 * SIDE]
    core, x, y = place(at_ref)
    for d in range(SIDE):
        for e in range(SIDE):
            y_d, x_e = lax.rem(y + SIDE - d, SIDE), lax.rem(x + SIDE - e, SIDE)
            out_ref[(y_d * SIDE + x_e) * CORES + core] = same[d][e]
            y_e, x_d = lax.rem(y + SIDE - e, SIDE), lax.rem(x + SIDE - d, SIDE)
            out_ref[(y_e * SIDE + x_d) * CORES + 1 - core] = other[d][e]


def exchange(at, towards_x, other):
    block, dtype = other.shape[1:], other.dtype
    islands = other.shape[0] * CORES
    line = jax.ShapeDtypeStruct((SIDE, *block), dtype)
    moved = 2 * other.size * 2

    def shift(v, dy, dx, dc):
        pairs = []
        for i in range(islands):
            y, rest = divmod(i, SIDE * CORES)
            x, c = divmod(rest, CORES)
            to = ((y + dy) % SIDE * SIDE + (x + dx) % SIDE) * CORES + (c + dc) % CORES
            pairs.append((i, to))
        return lax.ppermute(v, "island", pairs)

    def along(parts, dy, dx):
        out = list(parts)
        for d in (2, 1, 3):
            out[d] = shift(parts[d], dy * d, dx * d, 0)
        return out

    def relay(kernel, parts):
        return call(kernel, [line] * SIDE, [SMEM] + [VMEM] * len(parts), [VMEM] * SIDE, moved=moved)(at, *parts)

    other = shift(other, 0, 0, 1)
    same = along(towards_x, 0, 1)
    other = along(relay(split_other, [other]), 1, 0)
    same = along(relay(functools.partial(turn, 2), same), 1, 0)
    other = along(relay(functools.partial(turn, 1), other), 0, 1)
    return call(
        join_all,
        jax.ShapeDtypeStruct((islands, *block), dtype),
        [SMEM] + [VMEM] * (2 * SIDE),
        VMEM,
        moved=2 * moved,
    )(at, *same, *other)


def body(pseudo_grad, path_table, owner_place, outer_param, outer_momentum):
    islands = lax.axis_size("island")
    n = lax.axis_size("shard")
    levels = pseudo_grad.shape[1]
    narrow = pseudo_grad.shape[3]
    modules = owner_place.shape[0]
    per_level = modules // levels
    zr, width = outer_param.shape[1:]
    jrs, jcs = zr // TR, narrow // TC

    def swap(x):
        x = x.reshape(islands * n, levels, TR, TC)
        x = lax.all_to_all(x, ("island", "shard"), 0, 0, tiled=True)
        return x.reshape(islands, n, levels, TR, TC)

    at = lax.axis_index("island").astype(jnp.int32).reshape(1)
    row_block = pl.BlockSpec((1, levels, zr, narrow), lambda z: (0, 0, z, 0))
    z_tiles = pl.BlockSpec((islands, 1, levels, TR, TC), lambda z: (0, z, 0, 0, 0))
    packed = call(
        functools.partial(pack_kernel, jrs, jcs, levels),
        tiles(islands, n, levels),
        [row_block],
        z_tiles,
        grid=(n,),
        moved=4 << 20,
    )(pseudo_grad)
    grads = swap(packed)

    steps = 4
    band = pl.BlockSpec((1, zr // steps, width), lambda g: (0, g, 0))
    tile_band = pl.BlockSpec((islands // steps, n + 1, TR, TC), lambda g: (g, 0, 0, 0))
    leaving = [tiles(SIDE, n + 1, dtype=jnp.int16)] * SIDE + [tiles(islands // CORES, n + 1, dtype=jnp.int16)]
    *q, other = call(
        functools.partial(q_kernel, n, jcs),
        leaving,
        [SMEM, VMEM, VMEM],
        [VMEM] * (SIDE + 1),
        moved=6 << 20,
    )(at, outer_param, outer_momentum)
    q = exchange(at, q, other)

    sums, picked = call(
        functools.partial(reduce_kernel, n, islands, levels, per_level),
        [tiles(modules, n, dtype=jnp.float32), tiles(islands, n, levels)],
        [SMEM] * 2 + [VMEM] * 2,
        [VMEM] * 2,
        (pltpu.VMEM((modules, n, TR, TC), jnp.bfloat16), pltpu.SMEM((modules,), jnp.int32)),
        moved=8 << 20,
    )(path_table, owner_place, q, grads)
    arrived = swap(picked)

    *mean, other = call(
        functools.partial(mean_kernel, n, modules),
        leaving,
        [SMEM] * 2 + [VMEM],
        [VMEM] * (SIDE + 1),
        (pltpu.SMEM((modules,), jnp.int32),),
        moved=3 << 20,
    )(at, owner_place, sums)
    mean = exchange(at, mean, other)

    new_param, new_momentum = call(
        functools.partial(update_kernel, n, jrs // steps, jcs),
        [jax.ShapeDtypeStruct(outer_param.shape, jnp.float32)] * 2,
        [tile_band, band, band],
        [band, band],
        grid=(steps,),
        moved=10 << 20,
    )(mean, outer_param, outer_momentum)
    returned = call(
        functools.partial(unpack_kernel, jrs, jcs, levels),
        jax.ShapeDtypeStruct(pseudo_grad.shape, jnp.bfloat16),
        [z_tiles],
        row_block,
        grid=(n,),
        moved=4 << 20,
    )(arrived)
    return new_param, new_momentum, returned


def solution(mesh):
    placed = (
        P("island", None, None, "shard"),
        P(),
        P(),
        P("island", "shard", None),
        P("island", "shard", None),
    )
    return jax.shard_map(
        body,
        mesh=mesh,
        in_specs=placed,
        out_specs=(
            P("island", "shard", None),
            P("island", "shard", None),
            P("island", None, None, "shard"),
        ),
        check_vma=False,
    )
```

```python
import functools

import jax
import jax.numpy as jnp
from jax import lax
from jax.experimental import pallas as pl
from jax.experimental.pallas import tpu as pltpu
from jax.sharding import PartitionSpec as P

LEARN_RATE = 0.7
MOMENTUM_COEF = 0.9
Q_COEF = LEARN_RATE * MOMENTUM_COEF * MOMENTUM_COEF
G_COEF = LEARN_RATE * (1.0 + MOMENTUM_COEF)
LEAST = 1e-30
LIMIT = 32000.0
STEPS = 8.0
TR, TC = 16, 128
MIB = 1024 * 1024

SMEM = pl.BlockSpec(memory_space=pltpu.SMEM)
VMEM = pl.BlockSpec(memory_space=pltpu.VMEM)
ANY = pl.BlockSpec(memory_space=pl.ANY)
DMA = pltpu.SemaphoreType.DMA
copy = pltpu.make_async_copy


def call(kernel, out_shape, in_specs, out_specs, scratch=(), vmem=16, moved=0):
    return pl.pallas_call(
        kernel,
        out_shape=out_shape,
        in_specs=in_specs,
        out_specs=out_specs,
        scratch_shapes=scratch,
        compiler_params=pltpu.CompilerParams(vmem_limit_bytes=vmem * MIB),
        cost_estimate=pl.CostEstimate(flops=moved, bytes_accessed=moved, transcendentals=0),
    )


def tiles(*lead, dtype=jnp.bfloat16):
    return jax.ShapeDtypeStruct((*lead, TR, TC), dtype)


def stream(ins, work, outs):
    for c in ins:
        c.start()
    for k, c in enumerate(ins):
        c.wait()
        work(k)
        outs[k].start()
    for c in outs:
        c.wait()


def pack_kernel(n, zr, jrs, jcs, levels, x_ref, out_ref, rows_vm, tiles_vm, in_sem, out_sem):
    def work(z):
        for l in range(levels):
            for jr in range(jrs):
                for jc in range(jcs):
                    tile = rows_vm[z, l, jr * TR : (jr + 1) * TR, jc * TC : (jc + 1) * TC]
                    tiles_vm[z, jr * jcs + jc, l] = tile

    stream(
        [copy(x_ref.at[0, :, pl.ds(z * zr, zr)], rows_vm.at[z], in_sem.at[z]) for z in range(n)],
        work,
        [copy(tiles_vm.at[z], out_ref.at[:, z], out_sem.at[z]) for z in range(n)],
    )


def unpack_kernel(n, zr, jrs, jcs, levels, y_ref, out_ref, rows_vm, tiles_vm, in_sem, out_sem):
    def work(z):
        for l in range(levels):
            for jr in range(jrs):
                for jc in range(jcs):
                    tile = tiles_vm[z, jr * jcs + jc, l]
                    rows_vm[z, l, jr * TR : (jr + 1) * TR, jc * TC : (jc + 1) * TC] = tile

    stream(
        [copy(y_ref.at[:, z], tiles_vm.at[z], in_sem.at[z]) for z in range(n)],
        work,
        [copy(rows_vm.at[z], out_ref.at[0, :, pl.ds(z * zr, zr)], out_sem.at[z]) for z in range(n)],
    )


def store_coded(out, n, values):
    top = functools.reduce(jnp.maximum, [jnp.abs(v) for v in values])
    octave = jnp.ceil(jnp.log2(jnp.maximum(top, LEAST)) * STEPS)
    gain = LIMIT * jnp.exp2(octave * (-1.0 / STEPS))
    for s, v in enumerate(values):
        out[s] = jnp.round(v * gain).astype(jnp.int32).astype(jnp.int16)
    out[n] = octave.astype(jnp.int32).astype(jnp.int16)


def scale_of(code):
    return jnp.exp2(code.astype(jnp.int32).astype(jnp.float32) * (1.0 / STEPS)) * (1.0 / LIMIT)


def decoded(code, scale):
    return code.astype(jnp.int32).astype(jnp.float32) * scale


CORES, SIDE = 2, 4


def place(at_ref):
    at = at_ref[0]
    return at % CORES, at // CORES % SIDE, at // (CORES * SIDE)


def towards(at_ref, emit):
    core, x, _ = place(at_ref)
    for y in range(SIDE):
        for d in range(SIDE):
            emit(d, y, y, lax.rem(x + d, SIDE), core)
            emit(SIDE, y * SIDE + d, y, d, 1 - core)


def q_kernel(n, jcs, at_ref, p_ref, m_ref, *outs):
    def emit(d, slot, y, x, core):
        rows = pl.ds(pl.multiple_of((y * SIDE + x) * TR, TR), TR)
        cols = [pl.ds(pl.multiple_of((s * jcs + core) * TC, TC), TC) for s in range(n)]
        store_coded(outs[d].at[slot], n, [p_ref[0, rows, c] - Q_COEF * m_ref[0, rows, c] for c in cols])

    towards(at_ref, emit)


def update_kernel(n, jcs, at_ref, *refs):
    parts, (p_ref, m_ref, np_ref, nm_ref) = refs[: 2 * SIDE], refs[2 * SIDE : 2 * SIDE + 4]
    parts_vm, p_vm, m_vm, np_vm, nm_vm, part_sem, in_sem, out_sem = refs[2 * SIDE + 4 :]
    core, x, y = place(at_ref)
    deep = SIDE * TR
    bands = [pl.ds(pl.multiple_of(lax.rem(y + SIDE - a, SIDE) * deep, deep), deep) for a in range(SIDE)]
    g_in = [copy(parts[k], parts_vm.at[k], part_sem.at[k]) for k in range(2 * SIDE)]
    p_in = [copy(p_ref.at[0, bands[a]], p_vm.at[a], in_sem.at[0, a]) for a in range(SIDE)]
    m_in = [copy(m_ref.at[0, bands[a]], m_vm.at[a], in_sem.at[1, a]) for a in range(SIDE)]
    p_out = [copy(np_vm.at[a], np_ref.at[0, bands[a]], out_sem.at[0, a]) for a in range(SIDE)]
    m_out = [copy(nm_vm.at[a], nm_ref.at[0, bands[a]], out_sem.at[1, a]) for a in range(SIDE)]
    for c in g_in:
        c.start()
    for a in range(SIDE):
        p_in[a].start()
        m_in[a].start()
    for c in g_in:
        c.wait()
    for a in range(SIDE):
        p_in[a].wait()
        m_in[a].wait()
        for e in range(SIDE):
            rows = pl.ds(pl.multiple_of(lax.rem(x + SIDE - e, SIDE) * TR, TR), TR)
            for block, jc in ((parts_vm.at[a, e], core), (parts_vm.at[SIDE + e, a], 1 - core)):
                scale = scale_of(block[n])
                for s in range(n):
                    cols = pl.ds(pl.multiple_of((s * jcs + jc) * TC, TC), TC)
                    g = decoded(block[s], scale)
                    nm = MOMENTUM_COEF * m_vm[a, rows, cols] + g
                    nm_vm[a, rows, cols] = nm
                    np_vm[a, rows, cols] = p_vm[a, rows, cols] - LEARN_RATE * (g + MOMENTUM_COEF * nm)
        p_out[a].start()
        m_out[a].start()
    for c in p_out + m_out:
        c.wait()


def share_of(count):
    return jnp.full((TR, TC), 1.0, jnp.float32) / jnp.maximum(count, 1).astype(jnp.float32)


CHUNK = 4


def reduce_kernel(n, islands, levels, per_level, path_ref, owner_ref, q_ref, x_ref, sum_ref, pick_ref, *scratch):
    q_vm, x_vm, acc, new, pick_vm, cnt, q_sem, in_sem, out_sem, sum_sem = scratch
    pieces = [pl.ds(k * CHUNK, CHUNK) for k in range(islands // CHUNK)]
    ins = [copy(x_ref.at[p], x_vm.at[p], in_sem.at[k]) for k, p in enumerate(pieces)]
    outs = [copy(pick_vm.at[p], pick_ref.at[p], out_sem.at[k]) for k, p in enumerate(pieces)]
    q_in = copy(q_ref, q_vm, q_sem)
    sum_out = copy(acc, sum_ref, sum_sem)
    for c in ins:
        c.start()
    q_in.start()
    acc[...] = jnp.zeros_like(acc)
    for m in range(levels * per_level):
        cnt[m] = 0

    def add(i, carry):
        for l in range(levels):
            m = l * per_level + path_ref[i, l]
            cnt[m] = cnt[m] + 1
            for s in range(n):
                acc[m, s] += x_vm[i, s, l].astype(jnp.float32)
        return carry

    for k, c in enumerate(ins):
        c.wait()
        lax.fori_loop(k * CHUNK, (k + 1) * CHUNK, add, 0)
    sum_out.start()
    q_in.wait()

    def finish(m, carry):
        t = owner_ref[m]
        weight = G_COEF * share_of(cnt[m])
        scale = scale_of(q_vm[t, n])
        for s in range(n):
            new[m, s] = (decoded(q_vm[t, s], scale) - acc[m, s] * weight).astype(jnp.bfloat16)
        return carry

    lax.fori_loop(0, levels * per_level, finish, 0, unroll=2)

    def pick(i, carry):
        for l in range(levels):
            m = l * per_level + path_ref[i, l]
            for s in range(n):
                pick_vm[i, s, l] = new[m, s]
        return carry

    for k, c in enumerate(outs):
        lax.fori_loop(k * CHUNK, (k + 1) * CHUNK, pick, 0, unroll=2)
        c.start()
    for c in outs:
        c.wait()
    sum_out.wait()


def mean_kernel(n, islands, levels, per_level, at_ref, path_ref, owner_ref, sum_ref, *refs):
    outs, module, cnt = refs[: SIDE + 1], refs[SIDE + 1], refs[SIDE + 2]
    for m in range(levels * per_level):
        module[owner_ref[m]] = m
        cnt[m] = 0

    def add(i, carry):
        for l in range(levels):
            m = l * per_level + path_ref[i, l]
            cnt[m] = cnt[m] + 1
        return carry

    lax.fori_loop(0, islands, add, 0)

    def emit(d, slot, y, x, core):
        m = module[(y * SIDE + x) * CORES + core]
        share = share_of(cnt[m])
        store_coded(outs[d].at[slot], n, [sum_ref[m, s] * share for s in range(n)])

    towards(at_ref, emit)


def split_other(at_ref, other_ref, *outs):
    _, _, y = place(at_ref)
    for d in range(SIDE):
        for x in range(SIDE):
            outs[d][x] = other_ref[lax.rem(y + d, SIDE) * SIDE + x]


def turn(across, at_ref, *refs):
    ins, outs = refs[:SIDE], refs[SIDE:]
    mine = place(at_ref)[across]
    for d in range(SIDE):
        for e in range(SIDE):
            outs[d][e] = ins[e][lax.rem(mine + d, SIDE)]


def join_all(at_ref, *refs):
    same, other, out_ref = refs[:SIDE], refs[SIDE : 2 * SIDE], refs[2 * SIDE]
    core, x, y = place(at_ref)
    for d in range(SIDE):
        for e in range(SIDE):
            y_d, x_e = lax.rem(y + SIDE - d, SIDE), lax.rem(x + SIDE - e, SIDE)
            out_ref[(y_d * SIDE + x_e) * CORES + core] = same[d][e]
            y_e, x_d = lax.rem(y + SIDE - e, SIDE), lax.rem(x + SIDE - d, SIDE)
            out_ref[(y_e * SIDE + x_d) * CORES + 1 - core] = other[d][e]


def exchange(at, towards_x, other):
    block, dtype = other.shape[1:], other.dtype
    islands = other.shape[0] * CORES
    line = jax.ShapeDtypeStruct((SIDE, *block), dtype)
    moved = 2 * other.size * 2

    def shift(v, dy, dx, dc):
        pairs = []
        for i in range(islands):
            y, rest = divmod(i, SIDE * CORES)
            x, c = divmod(rest, CORES)
            to = ((y + dy) % SIDE * SIDE + (x + dx) % SIDE) * CORES + (c + dc) % CORES
            pairs.append((i, to))
        return lax.ppermute(v, "island", pairs)

    def along(parts, dy, dx):
        out = list(parts)
        for d in (2, 1, 3):
            out[d] = shift(parts[d], dy * d, dx * d, 0)
        return out

    def relay(kernel, parts):
        return call(kernel, [line] * SIDE, [SMEM] + [VMEM] * len(parts), [VMEM] * SIDE, moved=moved)(at, *parts)

    other = shift(other, 0, 0, 1)
    same = along(towards_x, 0, 1)
    other = along(relay(split_other, [other]), 1, 0)
    same = along(relay(functools.partial(turn, 2), same), 1, 0)
    other = along(relay(functools.partial(turn, 1), other), 0, 1)
    return [*same, *other]


def body(pseudo_grad, path_table, owner_place, outer_param, outer_momentum):
    islands = lax.axis_size("island")
    n = lax.axis_size("shard")
    levels = pseudo_grad.shape[1]
    narrow = pseudo_grad.shape[3]
    modules = owner_place.shape[0]
    per_level = modules // levels
    zr, width = outer_param.shape[1:]
    jrs, jcs = zr // TR, narrow // TC

    def swap(x):
        x = x.reshape(islands * n, levels, TR, TC)
        x = lax.all_to_all(x, ("island", "shard"), 0, 0, tiled=True)
        return x.reshape(islands, n, levels, TR, TC)

    at = lax.axis_index("island").astype(jnp.int32).reshape(1)
    in_rows = pltpu.VMEM((n, levels, zr, narrow), jnp.bfloat16)
    in_tiles = pltpu.VMEM((n, islands, levels, TR, TC), jnp.bfloat16)
    packed = call(
        functools.partial(pack_kernel, n, zr, jrs, jcs, levels),
        tiles(islands, n, levels),
        [ANY],
        ANY,
        (in_rows, in_tiles, DMA((n,)), DMA((n,))),
        vmem=63,
        moved=4 << 20,
    )(pseudo_grad)
    grads = swap(packed)

    leaving = [tiles(SIDE, n + 1, dtype=jnp.int16)] * SIDE + [tiles(islands // CORES, n + 1, dtype=jnp.int16)]
    *q, other = call(
        functools.partial(q_kernel, n, jcs),
        leaving,
        [SMEM, VMEM, VMEM],
        [VMEM] * (SIDE + 1),
        moved=6 << 20,
    )(at, outer_param, outer_momentum)
    q = call(
        join_all,
        tiles(islands, n + 1, dtype=jnp.int16),
        [SMEM] + [VMEM] * (2 * SIDE),
        VMEM,
        moved=4 << 20,
    )(at, *exchange(at, q, other))

    sums, picked = call(
        functools.partial(reduce_kernel, n, islands, levels, per_level),
        [tiles(modules, n, dtype=jnp.float32), tiles(islands, n, levels)],
        [SMEM] * 2 + [ANY] * 2,
        [ANY] * 2,
        (
            pltpu.VMEM((islands, n + 1, TR, TC), jnp.int16),
            pltpu.VMEM((islands, n, levels, TR, TC), jnp.bfloat16),
            pltpu.VMEM((modules, n, TR, TC), jnp.float32),
            pltpu.VMEM((modules, n, TR, TC), jnp.bfloat16),
            pltpu.VMEM((islands, n, levels, TR, TC), jnp.bfloat16),
            pltpu.SMEM((modules,), jnp.int32),
            DMA,
            DMA((islands // CHUNK,)),
            DMA((islands // CHUNK,)),
            DMA,
        ),
        vmem=63,
        moved=8 << 20,
    )(path_table, owner_place, q, grads)
    arrived = swap(picked)

    *mean, other = call(
        functools.partial(mean_kernel, n, islands, levels, per_level),
        leaving,
        [SMEM] * 3 + [VMEM],
        [VMEM] * (SIDE + 1),
        (pltpu.SMEM((modules,), jnp.int32),) * 2,
        moved=3 << 20,
    )(at, path_table, owner_place, sums)
    bands = pltpu.VMEM((SIDE, SIDE * TR, width), jnp.float32)
    new_param, new_momentum = call(
        functools.partial(update_kernel, n, jcs),
        [jax.ShapeDtypeStruct(outer_param.shape, jnp.float32)] * 2,
        [SMEM] + [ANY] * (2 * SIDE + 2),
        [ANY] * 2,
        (
            pltpu.VMEM((2 * SIDE, SIDE, n + 1, TR, TC), jnp.int16),
            *[bands] * 4,
            DMA((2 * SIDE,)),
            DMA((2, SIDE)),
            DMA((2, SIDE)),
        ),
        moved=10 << 20,
    )(at, *exchange(at, mean, other), outer_param, outer_momentum)
    returned = call(
        functools.partial(unpack_kernel, n, zr, jrs, jcs, levels),
        jax.ShapeDtypeStruct(pseudo_grad.shape, jnp.bfloat16),
        [ANY],
        ANY,
        (in_rows, in_tiles, DMA((n,)), DMA((n,))),
        vmem=63,
        moved=4 << 20,
    )(arrived)
    return new_param, new_momentum, returned


def solution(mesh):
    placed = (
        P("island", None, None, "shard"),
        P(),
        P(),
        P("island", "shard", None),
        P("island", "shard", None),
    )
    return jax.shard_map(
        body,
        mesh=mesh,
        in_specs=placed,
        out_specs=(
            P("island", "shard", None),
            P("island", "shard", None),
            P("island", None, None, "shard"),
        ),
        check_vma=False,
    )
```

```python
import functools

import jax
import jax.numpy as jnp
from jax import lax
from jax.experimental import pallas as pl
from jax.experimental.pallas import tpu as pltpu
from jax.sharding import PartitionSpec as P

LEARN_RATE = 0.7
MOMENTUM_COEF = 0.9
Q_COEF = LEARN_RATE * MOMENTUM_COEF * MOMENTUM_COEF
G_COEF = LEARN_RATE * (1.0 + MOMENTUM_COEF)
LEAST = 1e-30
LIMIT = 32000.0
STEPS = 8.0
TR, TC = 16, 128
MIB = 1024 * 1024

SMEM = pl.BlockSpec(memory_space=pltpu.SMEM)
VMEM = pl.BlockSpec(memory_space=pltpu.VMEM)
ANY = pl.BlockSpec(memory_space=pl.ANY)
DMA = pltpu.SemaphoreType.DMA
copy = pltpu.make_async_copy


def call(kernel, out_shape, in_specs, out_specs, scratch=(), vmem=16, moved=0):
    return pl.pallas_call(
        kernel,
        out_shape=out_shape,
        in_specs=in_specs,
        out_specs=out_specs,
        scratch_shapes=scratch,
        compiler_params=pltpu.CompilerParams(vmem_limit_bytes=vmem * MIB),
        cost_estimate=pl.CostEstimate(flops=moved, bytes_accessed=moved, transcendentals=0),
    )


def tiles(*lead, dtype=jnp.bfloat16):
    return jax.ShapeDtypeStruct((*lead, TR, TC), dtype)


def repack_kernel(n, jcs, levels, unpack, src_ref, dst_ref, sem):
    rows, packed = (dst_ref, src_ref) if unpack else (src_ref, dst_ref)
    moves = []
    for z in range(n):
        for l in range(levels):
            for jc in range(jcs):
                pair = (rows.at[l, z, :, :, pl.ds(jc * TC, TC)], packed.at[:, jc, z, l])
                src, dst = pair[::-1] if unpack else pair
                moves.append(copy(src, dst, sem.at[z, l, jc]))
    for c in moves:
        c.start()
    for c in moves:
        c.wait()


def store_coded(out, n, values):
    top = functools.reduce(jnp.maximum, [jnp.abs(v) for v in values])
    octave = jnp.ceil(jnp.log2(jnp.maximum(top, LEAST)) * STEPS)
    gain = LIMIT * jnp.exp2(octave * (-1.0 / STEPS))
    for s, v in enumerate(values):
        out[s] = jnp.round(v * gain).astype(jnp.int32).astype(jnp.int16)
    out[n] = octave.astype(jnp.int32).astype(jnp.int16)


def scale_of(code):
    return jnp.exp2(code.astype(jnp.int32).astype(jnp.float32) * (1.0 / STEPS)) * (1.0 / LIMIT)


def decoded(code, scale):
    return code.astype(jnp.int32).astype(jnp.float32) * scale


CORES, SIDE = 2, 4


def place(at_ref):
    at = at_ref[0]
    return at % CORES, at // CORES % SIDE, at // (CORES * SIDE)


def towards(at_ref, emit):
    core, x, _ = place(at_ref)
    for y in range(SIDE):
        for d in range(SIDE):
            emit(d, y, y, lax.rem(x + d, SIDE), core)
            emit(SIDE, y * SIDE + d, y, d, 1 - core)


def q_kernel(n, jcs, at_ref, p_ref, m_ref, *outs):
    def emit(d, slot, y, x, core):
        rows = pl.ds(pl.multiple_of((y * SIDE + x) * TR, TR), TR)
        cols = [pl.ds(pl.multiple_of((s * jcs + core) * TC, TC), TC) for s in range(n)]
        store_coded(outs[d].at[slot], n, [p_ref[0, rows, c] - Q_COEF * m_ref[0, rows, c] for c in cols])

    towards(at_ref, emit)


def update_kernel(n, jcs, at_ref, *refs):
    parts, (p_ref, m_ref, np_ref, nm_ref) = refs[: 2 * SIDE], refs[2 * SIDE : 2 * SIDE + 4]
    parts_vm, p_vm, m_vm, np_vm, nm_vm, part_sem, in_sem, out_sem = refs[2 * SIDE + 4 :]
    core, x, y = place(at_ref)
    deep = SIDE * TR
    bands = [pl.ds(pl.multiple_of(lax.rem(y + SIDE - a, SIDE) * deep, deep), deep) for a in range(SIDE)]
    g_in = [copy(parts[k], parts_vm.at[k], part_sem.at[k]) for k in range(2 * SIDE)]
    p_in = [copy(p_ref.at[0, bands[a]], p_vm.at[a], in_sem.at[0, a]) for a in range(SIDE)]
    m_in = [copy(m_ref.at[0, bands[a]], m_vm.at[a], in_sem.at[1, a]) for a in range(SIDE)]
    p_out = [copy(np_vm.at[a], np_ref.at[0, bands[a]], out_sem.at[0, a]) for a in range(SIDE)]
    m_out = [copy(nm_vm.at[a], nm_ref.at[0, bands[a]], out_sem.at[1, a]) for a in range(SIDE)]
    for c in g_in:
        c.start()
    for a in range(SIDE):
        p_in[a].start()
        m_in[a].start()
    for c in g_in:
        c.wait()
    for a in range(SIDE):
        p_in[a].wait()
        m_in[a].wait()
        for e in range(SIDE):
            rows = pl.ds(pl.multiple_of(lax.rem(x + SIDE - e, SIDE) * TR, TR), TR)
            for block, jc in ((parts_vm.at[a, e], core), (parts_vm.at[SIDE + e, a], 1 - core)):
                scale = scale_of(block[n])
                for s in range(n):
                    cols = pl.ds(pl.multiple_of((s * jcs + jc) * TC, TC), TC)
                    g = decoded(block[s], scale)
                    nm = MOMENTUM_COEF * m_vm[a, rows, cols] + g
                    nm_vm[a, rows, cols] = nm
                    np_vm[a, rows, cols] = p_vm[a, rows, cols] - LEARN_RATE * (g + MOMENTUM_COEF * nm)
        p_out[a].start()
        m_out[a].start()
    for c in p_out + m_out:
        c.wait()


def share_of(count):
    return jnp.full((TR, TC), 1.0, jnp.float32) / jnp.maximum(count, 1).astype(jnp.float32)


CHUNK = 4


def reduce_kernel(n, islands, levels, per_level, path_ref, owner_ref, q_ref, x_ref, sum_ref, pick_ref, *scratch):
    q_vm, x_vm, acc, new, pick_vm, cnt, q_sem, in_sem, out_sem, sum_sem = scratch
    pieces = [pl.ds(k * CHUNK, CHUNK) for k in range(islands // CHUNK)]
    ins = [copy(x_ref.at[p], x_vm.at[p], in_sem.at[k]) for k, p in enumerate(pieces)]
    outs = [copy(pick_vm.at[p], pick_ref.at[p], out_sem.at[k]) for k, p in enumerate(pieces)]
    q_in = copy(q_ref, q_vm, q_sem)
    sum_out = copy(acc, sum_ref, sum_sem)
    for c in ins:
        c.start()
    q_in.start()
    acc[...] = jnp.zeros_like(acc)
    for m in range(levels * per_level):
        cnt[m] = 0

    def add(i, carry):
        for l in range(levels):
            m = l * per_level + path_ref[i, l]
            cnt[m] = cnt[m] + 1
            for s in range(n):
                acc[m, s] += x_vm[i, s, l].astype(jnp.float32)
        return carry

    for k, c in enumerate(ins):
        c.wait()
        lax.fori_loop(k * CHUNK, (k + 1) * CHUNK, add, 0)
    sum_out.start()
    q_in.wait()

    def finish(m, carry):
        t = owner_ref[m]
        weight = G_COEF * share_of(cnt[m])
        scale = scale_of(q_vm[t, n])
        for s in range(n):
            new[m, s] = (decoded(q_vm[t, s], scale) - acc[m, s] * weight).astype(jnp.bfloat16)
        return carry

    lax.fori_loop(0, levels * per_level, finish, 0, unroll=2)

    def pick(i, carry):
        for l in range(levels):
            m = l * per_level + path_ref[i, l]
            for s in range(n):
                pick_vm[i, s, l] = new[m, s]
        return carry

    for k, c in enumerate(outs):
        lax.fori_loop(k * CHUNK, (k + 1) * CHUNK, pick, 0, unroll=2)
        c.start()
    for c in outs:
        c.wait()
    sum_out.wait()


def mean_kernel(n, islands, levels, per_level, at_ref, path_ref, owner_ref, sum_ref, *refs):
    outs, module, cnt = refs[: SIDE + 1], refs[SIDE + 1], refs[SIDE + 2]
    for m in range(levels * per_level):
        module[owner_ref[m]] = m
        cnt[m] = 0

    def add(i, carry):
        for l in range(levels):
            m = l * per_level + path_ref[i, l]
            cnt[m] = cnt[m] + 1
        return carry

    lax.fori_loop(0, islands, add, 0)

    def emit(d, slot, y, x, core):
        m = module[(y * SIDE + x) * CORES + core]
        share = share_of(cnt[m])
        store_coded(outs[d].at[slot], n, [sum_ref[m, s] * share for s in range(n)])

    towards(at_ref, emit)


def split_other(at_ref, other_ref, *outs):
    _, _, y = place(at_ref)
    for d in range(SIDE):
        for x in range(SIDE):
            outs[d][x] = other_ref[lax.rem(y + d, SIDE) * SIDE + x]


def turn(across, at_ref, *refs):
    ins, outs = refs[:SIDE], refs[SIDE:]
    mine = place(at_ref)[across]
    for d in range(SIDE):
        for e in range(SIDE):
            outs[d][e] = ins[e][lax.rem(mine + d, SIDE)]


def join_all(at_ref, *refs):
    same, other, out_ref = refs[:SIDE], refs[SIDE : 2 * SIDE], refs[2 * SIDE]
    core, x, y = place(at_ref)
    for d in range(SIDE):
        for e in range(SIDE):
            y_d, x_e = lax.rem(y + SIDE - d, SIDE), lax.rem(x + SIDE - e, SIDE)
            out_ref[(y_d * SIDE + x_e) * CORES + core] = same[d][e]
            y_e, x_d = lax.rem(y + SIDE - e, SIDE), lax.rem(x + SIDE - d, SIDE)
            out_ref[(y_e * SIDE + x_d) * CORES + 1 - core] = other[d][e]


def exchange(at, towards_x, other):
    block, dtype = other.shape[1:], other.dtype
    islands = other.shape[0] * CORES
    line = jax.ShapeDtypeStruct((SIDE, *block), dtype)
    moved = 2 * other.size * 2

    def shift(v, dy, dx, dc):
        pairs = []
        for i in range(islands):
            y, rest = divmod(i, SIDE * CORES)
            x, c = divmod(rest, CORES)
            to = ((y + dy) % SIDE * SIDE + (x + dx) % SIDE) * CORES + (c + dc) % CORES
            pairs.append((i, to))
        return lax.ppermute(v, "island", pairs)

    def along(parts, dy, dx):
        out = list(parts)
        for d in (2, 1, 3):
            out[d] = shift(parts[d], dy * d, dx * d, 0)
        return out

    def relay(kernel, parts):
        return call(kernel, [line] * SIDE, [SMEM] + [VMEM] * len(parts), [VMEM] * SIDE, moved=moved)(at, *parts)

    other = shift(other, 0, 0, 1)
    same = along(towards_x, 0, 1)
    other = along(relay(split_other, [other]), 1, 0)
    same = along(relay(functools.partial(turn, 2), same), 1, 0)
    other = along(relay(functools.partial(turn, 1), other), 0, 1)
    return [*same, *other]


def body(pseudo_grad, path_table, owner_place, outer_param, outer_momentum):
    islands = lax.axis_size("island")
    n = lax.axis_size("shard")
    levels = pseudo_grad.shape[1]
    narrow = pseudo_grad.shape[3]
    modules = owner_place.shape[0]
    per_level = modules // levels
    zr, width = outer_param.shape[1:]
    jrs, jcs = zr // TR, narrow // TC

    def swap(x):
        x = x.reshape(islands * n, levels, TR, TC)
        x = lax.all_to_all(x, ("island", "shard"), 0, 0, tiled=True)
        return x.reshape(islands, n, levels, TR, TC)

    at = lax.axis_index("island").astype(jnp.int32).reshape(1)
    in_rows = jax.ShapeDtypeStruct((levels, n, jrs, TR, narrow), jnp.bfloat16)
    in_tiles = tiles(jrs, jcs, n, levels)

    def repack(x, unpack):
        return call(
            functools.partial(repack_kernel, n, jcs, levels, unpack),
            in_rows if unpack else in_tiles,
            [ANY],
            ANY,
            (DMA((n, levels, jcs)),),
            vmem=63,
            moved=4 << 20,
        )(x.reshape((in_tiles if unpack else in_rows).shape))

    packed = repack(pseudo_grad, False).reshape(islands, n, levels, TR, TC)
    grads = swap(packed)

    leaving = [tiles(SIDE, n + 1, dtype=jnp.int16)] * SIDE + [tiles(islands // CORES, n + 1, dtype=jnp.int16)]
    *q, other = call(
        functools.partial(q_kernel, n, jcs),
        leaving,
        [SMEM, VMEM, VMEM],
        [VMEM] * (SIDE + 1),
        moved=6 << 20,
    )(at, outer_param, outer_momentum)
    q = call(
        join_all,
        tiles(islands, n + 1, dtype=jnp.int16),
        [SMEM] + [VMEM] * (2 * SIDE),
        VMEM,
        moved=4 << 20,
    )(at, *exchange(at, q, other))

    sums, picked = call(
        functools.partial(reduce_kernel, n, islands, levels, per_level),
        [tiles(modules, n, dtype=jnp.float32), tiles(islands, n, levels)],
        [SMEM] * 2 + [ANY] * 2,
        [ANY] * 2,
        (
            pltpu.VMEM((islands, n + 1, TR, TC), jnp.int16),
            pltpu.VMEM((islands, n, levels, TR, TC), jnp.bfloat16),
            pltpu.VMEM((modules, n, TR, TC), jnp.float32),
            pltpu.VMEM((modules, n, TR, TC), jnp.bfloat16),
            pltpu.VMEM((islands, n, levels, TR, TC), jnp.bfloat16),
            pltpu.SMEM((modules,), jnp.int32),
            DMA,
            DMA((islands // CHUNK,)),
            DMA((islands // CHUNK,)),
            DMA,
        ),
        vmem=63,
        moved=8 << 20,
    )(path_table, owner_place, q, grads)
    arrived = swap(picked)

    *mean, other = call(
        functools.partial(mean_kernel, n, islands, levels, per_level),
        leaving,
        [SMEM] * 3 + [VMEM],
        [VMEM] * (SIDE + 1),
        (pltpu.SMEM((modules,), jnp.int32),) * 2,
        moved=3 << 20,
    )(at, path_table, owner_place, sums)
    bands = pltpu.VMEM((SIDE, SIDE * TR, width), jnp.float32)
    new_param, new_momentum = call(
        functools.partial(update_kernel, n, jcs),
        [jax.ShapeDtypeStruct(outer_param.shape, jnp.float32)] * 2,
        [SMEM] + [ANY] * (2 * SIDE + 2),
        [ANY] * 2,
        (
            pltpu.VMEM((2 * SIDE, SIDE, n + 1, TR, TC), jnp.int16),
            *[bands] * 4,
            DMA((2 * SIDE,)),
            DMA((2, SIDE)),
            DMA((2, SIDE)),
        ),
        moved=10 << 20,
    )(at, *exchange(at, mean, other), outer_param, outer_momentum)
    returned = repack(arrived, True).reshape(pseudo_grad.shape)
    return new_param, new_momentum, returned


def solution(mesh):
    placed = (
        P("island", None, None, "shard"),
        P(),
        P(),
        P("island", "shard", None),
        P("island", "shard", None),
    )
    return jax.shard_map(
        body,
        mesh=mesh,
        in_specs=placed,
        out_specs=(
            P("island", "shard", None),
            P("island", "shard", None),
            P("island", None, None, "shard"),
        ),
        check_vma=False,
    )
```
